32 devices in a mesh: members: 2 (over x), cols: 16 (over z, y, core).
Axes of the slice: x: 2, y: 2, z: 4, core: 2. Of those that a mesh axis runs over, the one named last changes fastest.
Arguments:
- adj_in: float32 [128, 5, 32, 1024], P(('members', 'cols')), parts along dimension 0, may hold values from -4 to 5
- courant_x: float32 [128, 32, 1024], P(('members', 'cols')), parts along dimension 0, may hold values from 0.05 to 0.45
- courant_y: float32 [128, 32, 1024], P(('members', 'cols')), parts along dimension 0, may hold values from 0.05 to 0.45
- spread: float32 [64, 32, 1024], P('cols'), may hold values from 0.5 to 2
- corr_band: float32 [5, 32, 32], replicated, may hold values from 0 to 1.5, as said below
- jacobian: bfloat16 [4096, 160, 128], P(('members', 'cols')), parts along dimension 0, may hold values from -0.5 to 0.5
- departures: bfloat16 [4096, 128], P(('members', 'cols')), parts along dimension 0, may hold values from -6 to 6
- obs_owner: int32 [4096], P(('members', 'cols')), parts along dimension 0, may hold values from 0 to 15, as said below
- obs_cell: int32 [4096], P(('members', 'cols')), parts along dimension 0, may hold values from 0 to 4095
- obs_count: int32 [4096], P(('members', 'cols')), parts along dimension 0, may hold values from 32 to 128
Outputs:
- gradient: float32 [128, 5, 32, 1024], P(('members', 'cols')), parts along dimension 0
The draws below stay inside these ranges and needn't reach their ends.
There are 2 independent parts, one for each index of `members`. The reference program is written for one: setup_inputs(seed, part) draws one part's arguments, and reference() takes and returns one part's arrays. A program takes and returns all parts, laid end to end along the dimension named above; an argument that names none is the same for every part. Nothing has to cross between parts.
Inputs may be any that keep to these rules, and one draw needn't show every extreme that they name: corr_band is symmetric in its last two dimensions and zero more than 4 levels from the diagonal. `obs_owner`: among one device's 128 panels no tile is named more than 16 times; in every draw one tile is named exactly 16 times by every device's panels.
All inputs are finite; a program needn't handle non-finite values.
Results may differ from the reference program's by a relative error of at most 0.0003.
Values sent between devices are 32-bit elements; how exact they have to be, the bound alone decides.
A program may use at most 64 MiB of HBM per device.

```python
import math
import jax
import jax.numpy as jnp
from jax import lax

F = 5
CH = 128
L = 32
BAND = 4
STEPS = 8
BX = 4
NY = 1024
P_SIZE = 128
CAP = 16
NX = 64
PANELS = 2048
N_COLS = 16


def draw_adj_in(key, part):
    key = jax.random.fold_in(key, 1)
    rough = jax.random.truncated_normal(key, -4.0, 4.0, (NX, F, L, NY), jnp.float32)
    return rough


def draw_corr_band(key, part):
    key = jax.random.fold_in(key, 2)
    key_off, key_diag = jax.random.split(key)
    offdiag = jax.random.uniform(key_off, (F, L, L), jnp.float32, 0.1, 0.3)
    offdiag = 0.5 * (offdiag + jnp.swapaxes(offdiag, 1, 2))
    diagonal = jax.random.uniform(key_diag, (F, L, 1), jnp.float32, 1.0, 1.5)
    levels = jnp.arange(L)
    gap = jnp.abs(levels[:, None] - levels[None, :])
    return jnp.where(gap == 0, diagonal, jnp.where(gap <= BAND, offdiag, 0.0))


def draw_obs_owner(key, part):
    key = jax.random.fold_in(key, 3)
    key_star, key_rest = jax.random.split(key)
    star = jax.random.randint(key_star, (), 0, N_COLS)
    tiles = (jnp.arange(N_COLS) + star) % N_COLS
    slots = jnp.repeat(tiles, CAP, total_repeat_length=N_COLS * CAP)
    others = slots[CAP:]
    all_keys = jax.random.split(key_rest, 2 * N_COLS)

    def one_block(pick_key, order_key):
        picked = jax.random.permutation(pick_key, others)[:P_SIZE - CAP]
        block = jnp.concatenate([jnp.full((CAP,), star, jnp.int32), picked.astype(jnp.int32)])
        return jax.random.permutation(order_key, block)
    owners = jax.vmap(one_block)(all_keys[:N_COLS], all_keys[N_COLS:])
    return owners.reshape(-1).astype(jnp.int32)


def set_ends(result, own_key, least, top_value):
    longest = result.shape.index(max(result.shape))
    spots = []
    for shift in (0, 1):
        where = [jax.random.randint(jax.random.fold_in(own_key, axis), (), 0, length) for axis, length in enumerate(result.shape)]
        where[longest] = (where[longest] + shift) % result.shape[longest]
        spots.append(tuple(where))
    return result.at[spots[0]].set(least).at[spots[1]].set(top_value)


def block_levels(rng, dims, shards, low, high):
    gain, own = 1.0, jax.random.fold_in(rng, 6)
    for axis_at, shards_of in shards:
        draws = jnp.exp(jax.random.uniform(jax.random.fold_in(own, axis_at), (shards_of,), jnp.float32, low / len(shards), high / len(shards)))
        gain = gain * jnp.repeat(draws, dims[axis_at] // shards_of).reshape([-1 if axis == axis_at else 1 for axis in range(len(dims))])
    return gain


def bell_draw(stream_key, dims, scale, most, shards=(), kind=jnp.bfloat16):
    entries = scale * jax.random.normal(stream_key, dims, jnp.float32)
    if shards:
        entries = entries * block_levels(stream_key, dims, shards, -0.22, 0.18)
    return jnp.clip(entries, -most, most).astype(kind)


def setup_inputs(seed: int = 0, part: int = 0) -> dict:
    splits = jax.random.split(jax.random.key(seed), 11)
    part_splits = jax.random.split(jax.random.fold_in(splits[10], part), 11)
    adj_in = draw_adj_in(jax.random.fold_in(jax.random.fold_in(splits[10], part), 71), part)
    courant_x = jnp.clip(0.05 + 0.39999999 * jax.random.uniform(part_splits[1], (NX, L, NY), jnp.float32) ** block_levels(part_splits[1], (NX, L, NY), ((0, 16),), -0.2, 0.2), 0.05, 0.45)
    courant_y = jnp.clip(0.05 + 0.39999999 * jax.random.uniform(part_splits[2], (NX, L, NY), jnp.float32) ** block_levels(part_splits[2], (NX, L, NY), ((0, 16),), -0.2, 0.2), 0.05, 0.45)
    spread = jnp.clip(jnp.exp(math.log(2.0) - 1.3862944 * jax.random.uniform(splits[3], (NX, L, NY), jnp.float32) ** block_levels(splits[3], (NX, L, NY), ((0, 16),), -0.2, 0.2)), 0.5, 2.0)
    corr_band = draw_corr_band(jax.random.fold_in(splits[10], 71), part)
    jacobian = bell_draw(part_splits[5], (PANELS, F * L, CH), CH ** -0.5, 0.5, ((0, 16),))
    departures = bell_draw(part_splits[6], (PANELS, CH), 1.0, 6.0, ((0, 16),))
    obs_owner = draw_obs_owner(jax.random.fold_in(jax.random.fold_in(splits[10], part), 71), part)
    obs_cell = set_ends(jax.random.randint(part_splits[8], (PANELS,), 0, BX * NY), jax.random.fold_in(part_splits[8], 1), 0, (BX * NY) - 1).astype(jnp.int32)
    obs_count = set_ends(jax.random.randint(part_splits[9], (PANELS,), CH // 4, CH + 1), jax.random.fold_in(part_splits[9], 1), CH // 4, CH).astype(jnp.int32)
    return {"adj_in": adj_in, "courant_x": courant_x, "courant_y": courant_y, "spread": spread, "corr_band": corr_band, "jacobian": jacobian, "departures": departures, "obs_owner": obs_owner, "obs_cell": obs_cell, "obs_count": obs_count}


def advect_back(adjoint, courant_x, courant_y):
    ahead_x = jnp.roll(adjoint, -1, axis=0)
    ahead_y = jnp.roll(adjoint, -1, axis=3)
    return adjoint + courant_x[:, None] * (ahead_x - adjoint) + courant_y[:, None] * (ahead_y - adjoint)

def panel_grad(pair):
    return jnp.einsum('pkc,pc->pk', pair[0].astype(jnp.float32), pair[1].astype(jnp.float32), precision=lax.Precision.HIGHEST)

def reference(adj_in, courant_x, courant_y, spread, corr_band, jacobian, departures, obs_owner, obs_cell, obs_count):
    advected = adj_in
    for advect_step in range(STEPS):
        advected = advect_back(advected, courant_x, courant_y)
    channel = jnp.arange(CH, dtype=jnp.int32)
    masked = jnp.where(channel[None, :] < obs_count[:, None], departures, jnp.zeros((), departures.dtype))
    blocks_jac = jacobian.reshape(N_COLS, P_SIZE, F * L, CH)
    blocks_dep = masked.reshape(N_COLS, P_SIZE, CH)
    obs_grad = lax.map(panel_grad, (blocks_jac, blocks_dep)).reshape(PANELS, F, L)
    glob_x = (obs_owner * BX + obs_cell // NY).astype(jnp.int32)
    glob_y = (obs_cell % NY).astype(jnp.int32)
    increment = jnp.zeros_like(advected).at[glob_x, :, :, glob_y].add(obs_grad)
    total = advected + increment
    scaled = spread[:, None] * total
    mixed = jnp.einsum('flk,xfky->xfly', corr_band, scaled, precision=lax.Precision.HIGHEST)
    return spread[:, None] * mixed
```

```python
import functools
import jax
import jax.numpy as jnp
from jax import lax
from jax.experimental import pallas as pl
from jax.experimental.pallas import tpu as pltpu
from jax.sharding import PartitionSpec as P

STEPS = 8
SUB = 8


def pieces(value):
    high = value.astype(jnp.bfloat16)
    rest = value - high.astype(jnp.float32)
    middle = rest.astype(jnp.bfloat16)
    low = (rest - middle.astype(jnp.float32)).astype(jnp.bfloat16)
    return high, middle, low


def window_kernel(
    n_cols,
    cap,
    adj_hbm,
    cx_hbm,
    cy_hbm,
    spread_hbm,
    corr_hbm,
    jac_hbm,
    dep_hbm,
    owner_hbm,
    cell_hbm,
    count_hbm,
    out_hbm,
    state,
    history,
    border,
    cx,
    cy,
    spread,
    corr,
    jac,
    dep,
    owner,
    cell,
    count,
    masked,
    grad,
    send_slots,
    recv_slots,
    increment,
    result,
    local_sem,
    row_send_sem,
    row_recv_sem,
    slot_send_sem,
    slot_recv_sem,
    out_sem,
):
    rows, fields, levels, cells = state.shape
    panels, field_levels, channels = jac.shape
    slots, width = send_slots.shape
    me = lax.axis_index("cols")
    left = lax.rem(me + n_cols - 1, n_cols)

    barrier = pltpu.get_barrier_semaphore()

    @pl.loop(1, n_cols)
    def _(shift):
        pl.semaphore_signal(barrier, inc=1, device_id={"cols": lax.rem(me + shift, n_cols)})

    loads = [
        pltpu.make_async_copy(source, target, local_sem.at[number])
        for number, (source, target) in enumerate(
            [(adj_hbm.at[x], state.at[x]) for x in range(rows)]
            + [
                (cx_hbm, cx),
                (cy_hbm, cy),
                (dep_hbm, dep),
                (owner_hbm, owner),
                (cell_hbm, cell),
                (count_hbm, count),
                (jac_hbm, jac),
                (spread_hbm, spread),
                (corr_hbm, corr),
            ]
        )
    ]
    for load in loads:
        load.start()

    pl.semaphore_wait(barrier, n_cols - 1)

    def row_copy(time, field):
        source = adj_hbm.at[0, field] if time == 0 else history.at[time - 1, field]
        return pltpu.make_async_remote_copy(
            src_ref=source,
            dst_ref=border.at[time, field],
            send_sem=row_send_sem.at[time, field],
            recv_sem=row_recv_sem.at[time, field],
            device_id={"cols": left},
        )

    @pl.loop(0, fields)
    def _(field):
        row_copy(0, field).start()

    for load in loads[: rows + 2]:
        load.wait()

    def advance(x, strip, value, ahead):
        return (
            value
            + cx[x, strip] * (ahead - value)
            + cy[x, strip] * (pltpu.roll(value, cells - 1, 1) - value)
        )

    strips = [pl.ds(SUB * s, SUB) for s in range(levels // SUB)]

    for time in range(1, rows):

        @pl.loop(0, fields)
        def _(field):
            for strip in strips:
                for x in range(rows - time):
                    if x == 0 and time > 1:
                        value = history[time - 2, field, strip]
                    else:
                        value = state[x, field, strip]
                    new = advance(x, strip, value, state[x + 1, field, strip])
                    if x == 0:
                        history[time - 1, field, strip] = new
                    else:
                        state[x, field, strip] = new
            row_copy(time, field).start()

    for load in loads[rows + 2 :]:
        load.wait()
    first = lax.broadcasted_iota(jnp.int32, (panels, panels), 0)
    second = lax.broadcasted_iota(jnp.int32, (panels, panels), 1)

    def as_column(row):
        return jnp.sum(jnp.where(first == second, row, 0), axis=1, keepdims=True)

    lane = lax.broadcasted_iota(jnp.int32, (panels, channels), 1)
    masked[...] = jnp.where(lane < as_column(count[...]), dep[...].astype(jnp.float32), 0.0)
    grad[...] = jnp.zeros_like(grad)

    @pl.loop(0, panels // SUB)
    def _(group):
        start = pl.multiple_of(group * SUB, SUB)
        weights = masked[pl.ds(start, SUB), :].astype(jnp.bfloat16)
        row = lax.broadcasted_iota(jnp.int32, (SUB, field_levels), 0)
        total = jnp.zeros((SUB, field_levels), jnp.float32)
        for i in range(SUB):
            product = lax.dot_general(
                weights, jac[start + i], (((1,), (1,)), ((), ())), preferred_element_type=jnp.float32
            )
            total = jnp.where(row == i, product, total)
        grad[pl.ds(start, SUB), 0:field_levels] = total

    same = (as_column(owner[...]) == owner[...]) & (first < second)
    position = jnp.sum(same.astype(jnp.int32), axis=0, keepdims=True)
    slot = owner[...] * cap + position
    placing = slot == lax.broadcasted_iota(jnp.int32, (slots, panels), 0)
    placing_cell = jnp.sum(
        jnp.where(placing, (cell[...] + 1).astype(jnp.float32), 0.0), axis=1, keepdims=True
    )
    chosen = placing.astype(jnp.float32).astype(jnp.bfloat16)
    placed = sum(
        jnp.dot(chosen, piece, preferred_element_type=jnp.float32) for piece in pieces(grad[...])
    )
    column = lax.broadcasted_iota(jnp.int32, (slots, width), 1)
    send_slots[...] = jnp.where(column == field_levels, placing_cell, placed)

    def slot_block(ref, device):
        return ref.at[pl.ds(pl.multiple_of(device * cap, SUB), cap), :]

    def slot_send(shift):
        target = lax.rem(me + shift, n_cols)
        return pltpu.make_async_remote_copy(
            src_ref=slot_block(send_slots, target),
            dst_ref=slot_block(recv_slots, me),
            send_sem=slot_send_sem.at[shift],
            recv_sem=slot_recv_sem.at[shift],
            device_id={"cols": target},
        )

    def slot_receive(shift):
        return pltpu.make_async_remote_copy(
            src_ref=slot_block(send_slots, me),
            dst_ref=slot_block(recv_slots, lax.rem(me + n_cols - shift, n_cols)),
            send_sem=slot_send_sem.at[shift],
            recv_sem=slot_recv_sem.at[shift],
            device_id={"cols": left},
        )

    @pl.loop(1, n_cols)
    def _(shift):
        slot_send(shift).start()

    own = pl.ds(pl.multiple_of(me * cap, SUB), cap)
    recv_slots[own, :] = send_slots[own, :]

    def add_panels():
        @pl.loop(1, n_cols)
        def _(shift):
            slot_receive(shift).wait_recv()

        received = recv_slots[...]
        target = received[:, field_levels : field_levels + 1].astype(jnp.int32) - 1
        parts = pieces(jnp.transpose(received)[0:field_levels, :])
        for x in range(rows):
            y = lax.broadcasted_iota(jnp.int32, (slots, cells), 1) + x * cells
            hit = (target == y).astype(jnp.float32).astype(jnp.bfloat16)
            increment[x] = sum(
                jnp.dot(part, hit, preferred_element_type=jnp.float32) for part in parts
            )

    def finish(x, field):
        inside = pl.ds(pl.multiple_of(field * levels, SUB), levels)
        total = state[x, field] + increment[x, inside, :]
        mixed = jnp.dot(
            corr[field],
            spread[x] * total,
            precision=lax.Precision.HIGHEST,
            preferred_element_type=jnp.float32,
        )
        result[x, field] = spread[x] * mixed
        out_copy(x, field).start()

    def out_copy(x, field):
        return pltpu.make_async_copy(result.at[x, field], out_hbm.at[x, field], out_sem.at[x, field])

    for time in range(STEPS):
        if time + rows == STEPS:
            add_panels()
        active = [x for x in reversed(range(rows)) if time + rows - x <= STEPS]

        @pl.loop(0, fields)
        def _(field):
            row_copy(time, field).wait_recv()
            for strip in strips:
                ahead = border[time, field, strip]
                for x in active:
                    later = time + rows - x
                    if x == 0:
                        value = history[later - 2, field, strip]
                    else:
                        value = state[x, field, strip]
                    ahead = advance(x, strip, value, ahead)
                    if x == 0 and later < STEPS:
                        history[later - 1, field, strip] = ahead
                    else:
                        state[x, field, strip] = ahead
            if time + rows < STEPS:
                row_copy(time + rows, field).start()
            else:
                finish(time + rows - STEPS, field)

    @pl.loop(1, n_cols)
    def _(shift):
        slot_send(shift).wait_send()

    for time in range(STEPS):

        @pl.loop(0, fields)
        def _(field):
            row_copy(time, field).wait_send()

    for x in range(rows):

        @pl.loop(0, fields)
        def _(field):
            out_copy(x, field).wait()


def per_device(
    adj_in,
    courant_x,
    courant_y,
    spread,
    corr_band,
    jacobian,
    departures,
    obs_owner,
    obs_cell,
    obs_count,
):
    rows, fields, levels, cells = adj_in.shape
    panels, field_levels, channels = jacobian.shape
    n_cols = lax.axis_size("cols")
    cap = -(-(2 * panels // n_cols) // SUB) * SUB
    slots = n_cols * cap
    width = -(-(field_levels + 1) // 128) * 128
    anywhere = pl.BlockSpec(memory_space=pl.ANY)
    f32, i32 = jnp.float32, jnp.int32
    return pl.pallas_call(
        functools.partial(window_kernel, n_cols, cap),
        out_shape=jax.ShapeDtypeStruct(adj_in.shape, f32),
        in_specs=[anywhere] * 10,
        out_specs=anywhere,
        scratch_shapes=[
            pltpu.VMEM(adj_in.shape, f32),
            pltpu.VMEM((STEPS - 1, fields, levels, cells), f32),
            pltpu.VMEM((STEPS, fields, levels, cells), f32),
            pltpu.VMEM(courant_x.shape, f32),
            pltpu.VMEM(courant_y.shape, f32),
            pltpu.VMEM(spread.shape, f32),
            pltpu.VMEM(corr_band.shape, f32),
            pltpu.VMEM(jacobian.shape, jacobian.dtype),
            pltpu.VMEM(departures.shape, departures.dtype),
            pltpu.VMEM((1, panels), i32),
            pltpu.VMEM((1, panels), i32),
            pltpu.VMEM((1, panels), i32),
            pltpu.VMEM((panels, channels), f32),
            pltpu.VMEM((panels, width), f32),
            pltpu.VMEM((slots, width), f32),
            pltpu.VMEM((slots, width), f32),
            pltpu.VMEM((rows, field_levels, cells), f32),
            pltpu.VMEM(adj_in.shape, f32),
            pltpu.SemaphoreType.DMA((rows + 9,)),
            pltpu.SemaphoreType.DMA((STEPS, fields)),
            pltpu.SemaphoreType.DMA((STEPS, fields)),
            pltpu.SemaphoreType.DMA((n_cols,)),
            pltpu.SemaphoreType.DMA((n_cols,)),
            pltpu.SemaphoreType.DMA((rows, fields)),
        ],
        compiler_params=pltpu.CompilerParams(
            collective_id=0, has_side_effects=True, vmem_limit_bytes=48 * 1024 * 1024
        ),
    )(
        adj_in,
        courant_x,
        courant_y,
        spread,
        corr_band,
        jacobian,
        departures,
        obs_owner.reshape(1, panels),
        obs_cell.reshape(1, panels),
        obs_count.reshape(1, panels),
    )


def solution(mesh):
    in_specs = (
        P(("members", "cols"), None, None, None),
        P(("members", "cols"), None, None),
        P(("members", "cols"), None, None),
        P("cols", None, None),
        P(),
        P(("members", "cols"), None, None),
        P(("members", "cols"), None),
        P(("members", "cols")),
        P(("members", "cols")),
        P(("members", "cols")),
    )
    out_specs = P(("members", "cols"), None, None, None)
    return jax.shard_map(
        per_device, mesh=mesh, in_specs=in_specs, out_specs=out_specs, check_vma=False
    )
```

```python
import functools
import jax
import jax.numpy as jnp
from jax import lax
from jax.experimental import pallas as pl
from jax.experimental.pallas import tpu as pltpu
from jax.sharding import PartitionSpec as P

STEPS = 8
SUB = 8


def pieces(value):
    high = value.astype(jnp.bfloat16)
    rest = value - high.astype(jnp.float32)
    middle = rest.astype(jnp.bfloat16)
    low = (rest - middle.astype(jnp.float32)).astype(jnp.bfloat16)
    return high, middle, low


def window_kernel(
    n_cols,
    cap,
    adj_hbm,
    cx_hbm,
    cy_hbm,
    spread_hbm,
    corr_hbm,
    jac_hbm,
    dep_hbm,
    owner_hbm,
    cell_hbm,
    count_hbm,
    out_hbm,
    state,
    history,
    border,
    cx,
    cy,
    spread,
    corr,
    jac,
    dep,
    owner,
    cell,
    count,
    masked,
    grad,
    send_slots,
    recv_slots,
    increment,
    result,
    local_sem,
    row_send_sem,
    row_recv_sem,
    slot_send_sem,
    slot_recv_sem,
    out_sem,
):
    rows, fields, levels, cells = state.shape
    panels, field_levels, channels = jac.shape
    slots, width = send_slots.shape
    me = lax.axis_index("cols")
    left = lax.rem(me + n_cols - 1, n_cols)

    barrier = pltpu.get_barrier_semaphore()

    @pl.loop(1, n_cols)
    def _(shift):
        pl.semaphore_signal(barrier, inc=1, device_id={"cols": lax.rem(me + shift, n_cols)})

    loads = [
        pltpu.make_async_copy(source, target, local_sem.at[number])
        for number, (source, target) in enumerate(
            [(adj_hbm.at[x], state.at[x]) for x in range(rows)]
            + [
                (cx_hbm, cx),
                (cy_hbm, cy),
                (dep_hbm, dep),
                (owner_hbm, owner),
                (cell_hbm, cell),
                (count_hbm, count),
                (jac_hbm, jac),
                (spread_hbm, spread),
                (corr_hbm, corr),
            ]
        )
    ]
    for load in loads:
        load.start()

    pl.semaphore_wait(barrier, n_cols - 1)

    def row_copy(time, field):
        source = adj_hbm.at[0, field] if time == 0 else history.at[time - 1, field]
        return pltpu.make_async_remote_copy(
            src_ref=source,
            dst_ref=border.at[time, field],
            send_sem=row_send_sem.at[time, field],
            recv_sem=row_recv_sem.at[time, field],
            device_id={"cols": left},
        )

    @pl.loop(0, fields)
    def _(field):
        row_copy(0, field).start()

    for load in loads[: rows + 2]:
        load.wait()

    def advance(x, strip, value, ahead):
        return (
            value
            + cx[x, strip] * (ahead - value)
            + cy[x, strip] * (pltpu.roll(value, cells - 1, 1) - value)
        )

    strips = [pl.ds(SUB * s, SUB) for s in range(levels // SUB)]

    for time in range(1, rows):

        @pl.loop(0, fields)
        def _(field):
            for strip in strips:
                for x in range(rows - time):
                    if x == 0 and time > 1:
                        value = history[time - 2, field, strip]
                    else:
                        value = state[x, field, strip]
                    new = advance(x, strip, value, state[x + 1, field, strip])
                    if x == 0:
                        history[time - 1, field, strip] = new
                    else:
                        state[x, field, strip] = new
            if time < 1:
                row_copy(time, field).start()

    for load in loads[rows + 2 :]:
        load.wait()
    first = lax.broadcasted_iota(jnp.int32, (panels, panels), 0)
    second = lax.broadcasted_iota(jnp.int32, (panels, panels), 1)

    def as_column(row):
        return jnp.sum(jnp.where(first == second, row, 0), axis=1, keepdims=True)

    lane = lax.broadcasted_iota(jnp.int32, (panels, channels), 1)
    masked[...] = jnp.where(lane < as_column(count[...]), dep[...].astype(jnp.float32), 0.0)
    grad[...] = jnp.zeros_like(grad)

    @pl.loop(0, panels // SUB)
    def _(group):
        start = pl.multiple_of(group * SUB, SUB)
        weights = masked[pl.ds(start, SUB), :].astype(jnp.bfloat16)
        row = lax.broadcasted_iota(jnp.int32, (SUB, field_levels), 0)
        total = jnp.zeros((SUB, field_levels), jnp.float32)
        for i in range(SUB):
            product = lax.dot_general(
                weights, jac[start + i], (((1,), (1,)), ((), ())), preferred_element_type=jnp.float32
            )
            total = jnp.where(row == i, product, total)
        grad[pl.ds(start, SUB), 0:field_levels] = total

    same = (as_column(owner[...]) == owner[...]) & (first < second)
    position = jnp.sum(same.astype(jnp.int32), axis=0, keepdims=True)
    slot = owner[...] * cap + position
    placing = slot == lax.broadcasted_iota(jnp.int32, (slots, panels), 0)
    placing_cell = jnp.sum(
        jnp.where(placing, (cell[...] + 1).astype(jnp.float32), 0.0), axis=1, keepdims=True
    )
    chosen = placing.astype(jnp.float32).astype(jnp.bfloat16)
    placed = sum(
        jnp.dot(chosen, piece, preferred_element_type=jnp.float32) for piece in pieces(grad[...])
    )
    column = lax.broadcasted_iota(jnp.int32, (slots, width), 1)
    send_slots[...] = jnp.where(column == field_levels, placing_cell, placed)

    def slot_block(ref, device):
        return ref.at[pl.ds(pl.multiple_of(device * cap, SUB), cap), :]

    def slot_send(shift):
        target = lax.rem(me + shift, n_cols)
        return pltpu.make_async_remote_copy(
            src_ref=slot_block(send_slots, target),
            dst_ref=slot_block(recv_slots, me),
            send_sem=slot_send_sem.at[shift],
            recv_sem=slot_recv_sem.at[shift],
            device_id={"cols": target},
        )

    def slot_receive(shift):
        return pltpu.make_async_remote_copy(
            src_ref=slot_block(send_slots, me),
            dst_ref=slot_block(recv_slots, lax.rem(me + n_cols - shift, n_cols)),
            send_sem=slot_send_sem.at[shift],
            recv_sem=slot_recv_sem.at[shift],
            device_id={"cols": left},
        )

    @pl.loop(1, n_cols)
    def _(shift):
        slot_send(shift).start()

    own = pl.ds(pl.multiple_of(me * cap, SUB), cap)
    recv_slots[own, :] = send_slots[own, :]


    @pl.loop(1, n_cols)
    def _(shift):
        slot_receive(shift).wait_recv()

    @pl.loop(0, fields)
    def _(field):
        row_copy(1, field).start()

    @pl.loop(0, fields)
    def _(field):
        row_copy(2, field).start()

    @pl.loop(0, fields)
    def _(field):
        row_copy(3, field).start()

    def add_panels():
        received = recv_slots[...]
        target = received[:, field_levels : field_levels + 1].astype(jnp.int32) - 1
        parts = pieces(jnp.transpose(received)[0:field_levels, :])
        for x in range(rows):
            y = lax.broadcasted_iota(jnp.int32, (slots, cells), 1) + x * cells
            hit = (target == y).astype(jnp.float32).astype(jnp.bfloat16)
            increment[x] = sum(
                jnp.dot(part, hit, preferred_element_type=jnp.float32) for part in parts
            )

    def finish(x, field):
        inside = pl.ds(pl.multiple_of(field * levels, SUB), levels)
        total = state[x, field] + increment[x, inside, :]
        mixed = jnp.dot(
            corr[field],
            spread[x] * total,
            precision=lax.Precision.HIGHEST,
            preferred_element_type=jnp.float32,
        )
        result[x, field] = spread[x] * mixed
        out_copy(x, field).start()

    def out_copy(x, field):
        return pltpu.make_async_copy(result.at[x, field], out_hbm.at[x, field], out_sem.at[x, field])

    for time in range(STEPS):
        if time + rows == STEPS:
            add_panels()
        active = [x for x in reversed(range(rows)) if time + rows - x <= STEPS]

        @pl.loop(0, fields)
        def _(field):
            row_copy(time, field).wait_recv()
            for strip in strips:
                ahead = border[time, field, strip]
                for x in active:
                    later = time + rows - x
                    if x == 0:
                        value = history[later - 2, field, strip]
                    else:
                        value = state[x, field, strip]
                    ahead = advance(x, strip, value, ahead)
                    if x == 0 and later < STEPS:
                        history[later - 1, field, strip] = ahead
                    else:
                        state[x, field, strip] = ahead
            if time + rows < STEPS:
                row_copy(time + rows, field).start()
            else:
                finish(time + rows - STEPS, field)

    @pl.loop(1, n_cols)
    def _(shift):
        slot_send(shift).wait_send()

    for time in range(STEPS):

        @pl.loop(0, fields)
        def _(field):
            row_copy(time, field).wait_send()

    for x in range(rows):

        @pl.loop(0, fields)
        def _(field):
            out_copy(x, field).wait()


def per_device(
    adj_in,
    courant_x,
    courant_y,
    spread,
    corr_band,
    jacobian,
    departures,
    obs_owner,
    obs_cell,
    obs_count,
):
    rows, fields, levels, cells = adj_in.shape
    panels, field_levels, channels = jacobian.shape
    n_cols = lax.axis_size("cols")
    cap = -(-(2 * panels // n_cols) // SUB) * SUB
    slots = n_cols * cap
    width = -(-(field_levels + 1) // 128) * 128
    anywhere = pl.BlockSpec(memory_space=pl.ANY)
    f32, i32 = jnp.float32, jnp.int32
    return pl.pallas_call(
        functools.partial(window_kernel, n_cols, cap),
        out_shape=jax.ShapeDtypeStruct(adj_in.shape, f32),
        in_specs=[anywhere] * 10,
        out_specs=anywhere,
        scratch_shapes=[
            pltpu.VMEM(adj_in.shape, f32),
            pltpu.VMEM((STEPS - 1, fields, levels, cells), f32),
            pltpu.VMEM((STEPS, fields, levels, cells), f32),
            pltpu.VMEM(courant_x.shape, f32),
            pltpu.VMEM(courant_y.shape, f32),
            pltpu.VMEM(spread.shape, f32),
            pltpu.VMEM(corr_band.shape, f32),
            pltpu.VMEM(jacobian.shape, jacobian.dtype),
            pltpu.VMEM(departures.shape, departures.dtype),
            pltpu.VMEM((1, panels), i32),
            pltpu.VMEM((1, panels), i32),
            pltpu.VMEM((1, panels), i32),
            pltpu.VMEM((panels, channels), f32),
            pltpu.VMEM((panels, width), f32),
            pltpu.VMEM((slots, width), f32),
            pltpu.VMEM((slots, width), f32),
            pltpu.VMEM((rows, field_levels, cells), f32),
            pltpu.VMEM(adj_in.shape, f32),
            pltpu.SemaphoreType.DMA((rows + 9,)),
            pltpu.SemaphoreType.DMA((STEPS, fields)),
            pltpu.SemaphoreType.DMA((STEPS, fields)),
            pltpu.SemaphoreType.DMA((n_cols,)),
            pltpu.SemaphoreType.DMA((n_cols,)),
            pltpu.SemaphoreType.DMA((rows, fields)),
        ],
        compiler_params=pltpu.CompilerParams(
            collective_id=0, has_side_effects=True, vmem_limit_bytes=48 * 1024 * 1024
        ),
    )(*[pltpu.with_memory_space_constraint(v, pltpu.HBM) for v in (
        adj_in,
        courant_x,
        courant_y,
        spread,
        corr_band,
        jacobian,
        departures,
        obs_owner.reshape(1, panels),
        obs_cell.reshape(1, panels),
        obs_count.reshape(1, panels),
)]
    )


def solution(mesh):
    in_specs = (
        P(("members", "cols"), None, None, None),
        P(("members", "cols"), None, None),
        P(("members", "cols"), None, None),
        P("cols", None, None),
        P(),
        P(("members", "cols"), None, None),
        P(("members", "cols"), None),
        P(("members", "cols")),
        P(("members", "cols")),
        P(("members", "cols")),
    )
    out_specs = P(("members", "cols"), None, None, None)
    return jax.shard_map(
        per_device, mesh=mesh, in_specs=in_specs, out_specs=out_specs, check_vma=False
    )
```

```python
import functools
import jax
import jax.numpy as jnp
from jax import lax
from jax.experimental import pallas as pl
from jax.experimental.pallas import tpu as pltpu
from jax.sharding import PartitionSpec as P

STEPS = 8
SUB = 8


def pieces(value):
    high = value.astype(jnp.bfloat16)
    rest = value - high.astype(jnp.float32)
    middle = rest.astype(jnp.bfloat16)
    low = (rest - middle.astype(jnp.float32)).astype(jnp.bfloat16)
    return high, middle, low


def window_kernel(
    n_cols,
    cap,
    adj_hbm,
    cx_hbm,
    cy_hbm,
    spread_hbm,
    corr_hbm,
    jac_hbm,
    dep_hbm,
    owner_hbm,
    cell_hbm,
    count_hbm,
    out_hbm,
    state,
    history,
    border,
    cx,
    cy,
    spread,
    corr,
    jac,
    dep,
    owner,
    cell,
    count,
    masked,
    grad,
    send_slots,
    recv_slots,
    increment,
    result,
    local_sem,
    row_send_sem,
    row_recv_sem,
    slot_send_sem,
    slot_recv_sem,
    out_sem,
):
    rows, fields, levels, cells = state.shape
    panels, field_levels, channels = jac.shape
    slots, width = send_slots.shape
    me = lax.axis_index("cols")
    left = lax.rem(me + n_cols - 1, n_cols)

    barrier = pltpu.get_barrier_semaphore()

    @pl.loop(1, n_cols)
    def _(shift):
        pl.semaphore_signal(barrier, inc=1, device_id={"cols": lax.rem(me + shift, n_cols)})

    loads = [
        pltpu.make_async_copy(source, target, local_sem.at[number])
        for number, (source, target) in enumerate(
            [(adj_hbm.at[x], state.at[x]) for x in range(rows)]
            + [
                (cx_hbm, cx),
                (cy_hbm, cy),
                (dep_hbm, dep),
                (owner_hbm, owner),
                (cell_hbm, cell),
                (count_hbm, count),
                (jac_hbm, jac),
                (spread_hbm, spread),
                (corr_hbm, corr),
            ]
        )
    ]
    for load in loads:
        load.start()

    pl.semaphore_wait(barrier, n_cols - 1)

    def row_copy(time, field):
        source = adj_hbm.at[0, field] if time == 0 else history.at[time - 1, field]
        return pltpu.make_async_remote_copy(
            src_ref=source,
            dst_ref=border.at[time, field],
            send_sem=row_send_sem.at[time, field],
            recv_sem=row_recv_sem.at[time, field],
            device_id={"cols": left},
        )

    @pl.loop(0, fields)
    def _(field):
        row_copy(0, field).start()

    for load in loads[: rows + 2]:
        load.wait()

    def advance(x, strip, value, ahead):
        return (
            value
            + cx[x, strip] * (ahead - value)
            + cy[x, strip] * (pltpu.roll(value, cells - 1, 1) - value)
        )

    strips = [pl.ds(SUB * s, SUB) for s in range(levels // SUB)]

    for time in range(1, rows):

        @pl.loop(0, fields)
        def _(field):
            for strip in strips:
                for x in range(rows - time):
                    if x == 0 and time > 1:
                        value = history[time - 2, field, strip]
                    else:
                        value = state[x, field, strip]
                    new = advance(x, strip, value, state[x + 1, field, strip])
                    if x == 0:
                        history[time - 1, field, strip] = new
                    else:
                        state[x, field, strip] = new
            if time < 1:
                row_copy(time, field).start()

    for load in loads[rows + 2 :]:
        load.wait()
    first = lax.broadcasted_iota(jnp.int32, (panels, panels), 0)
    second = lax.broadcasted_iota(jnp.int32, (panels, panels), 1)

    def as_column(row):
        return jnp.sum(jnp.where(first == second, row, 0), axis=1, keepdims=True)

    lane = lax.broadcasted_iota(jnp.int32, (panels, channels), 1)
    masked[...] = jnp.where(lane < as_column(count[...]), dep[...].astype(jnp.float32), 0.0)
    grad[...] = jnp.zeros_like(grad)

    @pl.loop(0, panels // SUB)
    def _(group):
        start = pl.multiple_of(group * SUB, SUB)
        weights = masked[pl.ds(start, SUB), :].astype(jnp.bfloat16)
        row = lax.broadcasted_iota(jnp.int32, (SUB, field_levels), 0)
        total = jnp.zeros((SUB, field_levels), jnp.float32)
        for i in range(SUB):
            product = lax.dot_general(
                weights, jac[start + i], (((1,), (1,)), ((), ())), preferred_element_type=jnp.float32
            )
            total = jnp.where(row == i, product, total)
        grad[pl.ds(start, SUB), 0:field_levels] = total

    same = (as_column(owner[...]) == owner[...]) & (first < second)
    position = jnp.sum(same.astype(jnp.int32), axis=0, keepdims=True)
    slot = owner[...] * cap + position
    placing = slot == lax.broadcasted_iota(jnp.int32, (slots, panels), 0)
    placing_cell = jnp.sum(
        jnp.where(placing, (cell[...] + 1).astype(jnp.float32), 0.0), axis=1, keepdims=True
    )
    chosen = placing.astype(jnp.float32).astype(jnp.bfloat16)
    placed = sum(
        jnp.dot(chosen, piece, preferred_element_type=jnp.float32) for piece in pieces(grad[...])
    )
    column = lax.broadcasted_iota(jnp.int32, (slots, width), 1)
    send_slots[...] = jnp.where(column == field_levels, placing_cell, placed)

    def slot_block(ref, device):
        return ref.at[pl.ds(pl.multiple_of(device * cap, SUB), cap), :]

    def slot_send(shift):
        target = lax.rem(me + shift, n_cols)
        return pltpu.make_async_remote_copy(
            src_ref=slot_block(send_slots, target),
            dst_ref=slot_block(recv_slots, me),
            send_sem=slot_send_sem.at[shift],
            recv_sem=slot_recv_sem.at[shift],
            device_id={"cols": target},
        )

    def slot_receive(shift):
        return pltpu.make_async_remote_copy(
            src_ref=slot_block(send_slots, me),
            dst_ref=slot_block(recv_slots, lax.rem(me + n_cols - shift, n_cols)),
            send_sem=slot_send_sem.at[shift],
            recv_sem=slot_recv_sem.at[shift],
            device_id={"cols": left},
        )

    @pl.loop(1, n_cols)
    def _(shift):
        slot_send(shift).start()

    own = pl.ds(pl.multiple_of(me * cap, SUB), cap)
    recv_slots[own, :] = send_slots[own, :]


    patient = me == 0

    def wait_for_slots():
        @pl.loop(1, n_cols)
        def _(shift):
            slot_receive(shift).wait_recv()

    pl.when(patient)(wait_for_slots)

    @pl.loop(0, fields)
    def _(field):
        row_copy(1, field).start()

    @pl.loop(0, fields)
    def _(field):
        row_copy(2, field).start()

    @pl.loop(0, fields)
    def _(field):
        row_copy(3, field).start()

    def add_panels():
        pl.when(jnp.logical_not(patient))(wait_for_slots)
        received = recv_slots[...]
        target = received[:, field_levels : field_levels + 1].astype(jnp.int32) - 1
        parts = pieces(jnp.transpose(received)[0:field_levels, :])
        for x in range(rows):
            y = lax.broadcasted_iota(jnp.int32, (slots, cells), 1) + x * cells
            hit = (target == y).astype(jnp.float32).astype(jnp.bfloat16)
            increment[x] = sum(
                jnp.dot(part, hit, preferred_element_type=jnp.float32) for part in parts
            )

    def finish(x, field):
        inside = pl.ds(pl.multiple_of(field * levels, SUB), levels)
        total = state[x, field] + increment[x, inside, :]
        mixed = jnp.dot(
            corr[field],
            spread[x] * total,
            precision=lax.Precision.HIGHEST,
            preferred_element_type=jnp.float32,
        )
        result[x, field] = spread[x] * mixed
        out_copy(x, field).start()

    def out_copy(x, field):
        return pltpu.make_async_copy(result.at[x, field], out_hbm.at[x, field], out_sem.at[x, field])

    for time in range(STEPS):
        if time + rows == STEPS:
            add_panels()
        active = [x for x in reversed(range(rows)) if time + rows - x <= STEPS]

        @pl.loop(0, fields)
        def _(field):
            row_copy(time, field).wait_recv()
            for strip in strips:
                ahead = border[time, field, strip]
                for x in active:
                    later = time + rows - x
                    if x == 0:
                        value = history[later - 2, field, strip]
                    else:
                        value = state[x, field, strip]
                    ahead = advance(x, strip, value, ahead)
                    if x == 0 and later < STEPS:
                        history[later - 1, field, strip] = ahead
                    else:
                        state[x, field, strip] = ahead
            if time + rows < STEPS:
                row_copy(time + rows, field).start()
            else:
                finish(time + rows - STEPS, field)

    @pl.loop(1, n_cols)
    def _(shift):
        slot_send(shift).wait_send()

    for time in range(STEPS):

        @pl.loop(0, fields)
        def _(field):
            row_copy(time, field).wait_send()

    for x in range(rows):

        @pl.loop(0, fields)
        def _(field):
            out_copy(x, field).wait()


def per_device(
    adj_in,
    courant_x,
    courant_y,
    spread,
    corr_band,
    jacobian,
    departures,
    obs_owner,
    obs_cell,
    obs_count,
):
    rows, fields, levels, cells = adj_in.shape
    panels, field_levels, channels = jacobian.shape
    n_cols = lax.axis_size("cols")
    cap = -(-(2 * panels // n_cols) // SUB) * SUB
    slots = n_cols * cap
    width = -(-(field_levels + 1) // 128) * 128
    anywhere = pl.BlockSpec(memory_space=pl.ANY)
    f32, i32 = jnp.float32, jnp.int32
    return pl.pallas_call(
        functools.partial(window_kernel, n_cols, cap),
        out_shape=jax.ShapeDtypeStruct(adj_in.shape, f32),
        in_specs=[anywhere] * 10,
        out_specs=anywhere,
        scratch_shapes=[
            pltpu.VMEM(adj_in.shape, f32),
            pltpu.VMEM((STEPS - 1, fields, levels, cells), f32),
            pltpu.VMEM((STEPS, fields, levels, cells), f32),
            pltpu.VMEM(courant_x.shape, f32),
            pltpu.VMEM(courant_y.shape, f32),
            pltpu.VMEM(spread.shape, f32),
            pltpu.VMEM(corr_band.shape, f32),
            pltpu.VMEM(jacobian.shape, jacobian.dtype),
            pltpu.VMEM(departures.shape, departures.dtype),
            pltpu.VMEM((1, panels), i32),
            pltpu.VMEM((1, panels), i32),
            pltpu.VMEM((1, panels), i32),
            pltpu.VMEM((panels, channels), f32),
            pltpu.VMEM((panels, width), f32),
            pltpu.VMEM((slots, width), f32),
            pltpu.VMEM((slots, width), f32),
            pltpu.VMEM((rows, field_levels, cells), f32),
            pltpu.VMEM(adj_in.shape, f32),
            pltpu.SemaphoreType.DMA((rows + 9,)),
            pltpu.SemaphoreType.DMA((STEPS, fields)),
            pltpu.SemaphoreType.DMA((STEPS, fields)),
            pltpu.SemaphoreType.DMA((n_cols,)),
            pltpu.SemaphoreType.DMA((n_cols,)),
            pltpu.SemaphoreType.DMA((rows, fields)),
        ],
        compiler_params=pltpu.CompilerParams(
            collective_id=0, has_side_effects=True, vmem_limit_bytes=48 * 1024 * 1024
        ),
    )(*[pltpu.with_memory_space_constraint(v, pltpu.HBM) for v in (
        adj_in,
        courant_x,
        courant_y,
        spread,
        corr_band,
        jacobian,
        departures,
        obs_owner.reshape(1, panels),
        obs_cell.reshape(1, panels),
        obs_count.reshape(1, panels),
)]
    )


def solution(mesh):
    in_specs = (
        P(("members", "cols"), None, None, None),
        P(("members", "cols"), None, None),
        P(("members", "cols"), None, None),
        P("cols", None, None),
        P(),
        P(("members", "cols"), None, None),
        P(("members", "cols"), None),
        P(("members", "cols")),
        P(("members", "cols")),
        P(("members", "cols")),
    )
    out_specs = P(("members", "cols"), None, None, None)
    return jax.shard_map(
        per_device, mesh=mesh, in_specs=in_specs, out_specs=out_specs, check_vma=False
    )
```

```python
import functools
import jax
import jax.numpy as jnp
from jax import lax
from jax.experimental import pallas as pl
from jax.experimental.pallas import tpu as pltpu
from jax.sharding import PartitionSpec as P

STEPS = 8
SUB = 8


def pieces(value):
    high = value.astype(jnp.bfloat16)
    rest = value - high.astype(jnp.float32)
    middle = rest.astype(jnp.bfloat16)
    low = (rest - middle.astype(jnp.float32)).astype(jnp.bfloat16)
    return high, middle, low


def window_kernel(
    n_cols,
    cap,
    adj_hbm,
    cx_hbm,
    cy_hbm,
    spread_hbm,
    corr_hbm,
    jac_hbm,
    dep_hbm,
    owner_hbm,
    cell_hbm,
    count_hbm,
    out_hbm,
    state,
    history,
    border,
    cx,
    cy,
    spread,
    corr,
    jac,
    dep,
    owner,
    cell,
    count,
    masked,
    grad,
    send_slots,
    recv_slots,
    increment,
    result,
    local_sem,
    row_send_sem,
    row_recv_sem,
    slot_send_sem,
    slot_recv_sem,
    out_sem,
):
    rows, fields, levels, cells = state.shape
    panels, field_levels, channels = jac.shape
    slots, width = n_cols * cap, grad.shape[1]
    fold = 2 if cap % (2 * SUB) == 0 else 1
    short = cap // fold
    me = lax.axis_index("cols")
    left = lax.rem(me + n_cols - 1, n_cols)

    barrier = pltpu.get_barrier_semaphore()

    @pl.loop(1, n_cols)
    def _(shift):
        pl.semaphore_signal(barrier, inc=1, device_id={"cols": lax.rem(me + shift, n_cols)})

    loads = [
        pltpu.make_async_copy(source, target, local_sem.at[number])
        for number, (source, target) in enumerate(
            [(adj_hbm.at[x], state.at[x]) for x in range(rows)]
            + [
                (cx_hbm, cx),
                (cy_hbm, cy),
                (dep_hbm, dep),
                (owner_hbm, owner),
                (cell_hbm, cell),
                (count_hbm, count),
                (jac_hbm, jac),
                (spread_hbm, spread),
                (corr_hbm, corr),
            ]
        )
    ]
    for load in loads:
        load.start()

    pl.semaphore_wait(barrier, n_cols - 1)

    def row_copy(time, field):
        source = adj_hbm.at[0, field] if time == 0 else history.at[time - 1, field]
        return pltpu.make_async_remote_copy(
            src_ref=source,
            dst_ref=border.at[time, field],
            send_sem=row_send_sem.at[time, field],
            recv_sem=row_recv_sem.at[time, field],
            device_id={"cols": left},
        )

    @pl.loop(0, fields)
    def _(field):
        row_copy(0, field).start()

    for load in loads[: rows + 2]:
        load.wait()

    def advance(x, strip, value, ahead):
        return (
            value
            + cx[x, strip] * (ahead - value)
            + cy[x, strip] * (pltpu.roll(value, cells - 1, 1) - value)
        )

    strips = [pl.ds(SUB * s, SUB) for s in range(levels // SUB)]

    for time in range(1, rows):

        @pl.loop(0, fields)
        def _(field):
            for strip in strips:
                for x in range(rows - time):
                    if x == 0 and time > 1:
                        value = history[time - 2, field, strip]
                    else:
                        value = state[x, field, strip]
                    new = advance(x, strip, value, state[x + 1, field, strip])
                    if x == 0:
                        history[time - 1, field, strip] = new
                    else:
                        state[x, field, strip] = new
            if time < 1:
                row_copy(time, field).start()

    for load in loads[rows + 2 :]:
        load.wait()
    first = lax.broadcasted_iota(jnp.int32, (panels, panels), 0)
    second = lax.broadcasted_iota(jnp.int32, (panels, panels), 1)

    def as_column(row):
        return jnp.sum(jnp.where(first == second, row, 0), axis=1, keepdims=True)

    lane = lax.broadcasted_iota(jnp.int32, (panels, channels), 1)
    masked[...] = jnp.where(lane < as_column(count[...]), dep[...].astype(jnp.float32), 0.0)
    grad[...] = jnp.zeros_like(grad)

    @pl.loop(0, panels // SUB)
    def _(group):
        start = pl.multiple_of(group * SUB, SUB)
        weights = masked[pl.ds(start, SUB), :].astype(jnp.bfloat16)
        row = lax.broadcasted_iota(jnp.int32, (SUB, field_levels), 0)
        total = jnp.zeros((SUB, field_levels), jnp.float32)
        for i in range(SUB):
            product = lax.dot_general(
                weights, jac[start + i], (((1,), (1,)), ((), ())), preferred_element_type=jnp.float32
            )
            total = jnp.where(row == i, product, total)
        grad[pl.ds(start, SUB), 0:field_levels] = total

    same = (as_column(owner[...]) == owner[...]) & (first < second)
    position = jnp.sum(same.astype(jnp.int32), axis=0, keepdims=True)
    slot = owner[...] * cap + position
    placing = slot == lax.broadcasted_iota(jnp.int32, (slots, panels), 0)
    placing_cell = jnp.sum(
        jnp.where(placing, (cell[...] + 1).astype(jnp.float32), 0.0), axis=1, keepdims=True
    )
    chosen = placing.astype(jnp.float32).astype(jnp.bfloat16)
    placed = sum(
        jnp.dot(chosen, piece, preferred_element_type=jnp.float32) for piece in pieces(grad[...])
    )
    column = lax.broadcasted_iota(jnp.int32, (slots, width), 1)
    placed = jnp.where(column == field_levels, placing_cell, placed)
    wide = placed[:, 0:128].reshape(n_cols, cap, 128)
    rest = placed[:, 128:256]
    if fold == 2:
        pairs = rest.reshape(n_cols, 2, short, 128)
        upper = pltpu.roll(pairs[:, 1].reshape(n_cols * short, 128), 64, 1)
        rest = pairs[:, 0].reshape(n_cols * short, 128) + upper
    send_slots[:, 0:cap, :] = wide
    send_slots[:, cap : cap + short, :] = rest.reshape(n_cols, short, 128)

    def slot_block(ref, device):
        return ref.at[device]

    def slot_send(shift):
        target = lax.rem(me + shift, n_cols)
        return pltpu.make_async_remote_copy(
            src_ref=slot_block(send_slots, target),
            dst_ref=slot_block(recv_slots, me),
            send_sem=slot_send_sem.at[shift],
            recv_sem=slot_recv_sem.at[shift],
            device_id={"cols": target},
        )

    def slot_receive(shift):
        return pltpu.make_async_remote_copy(
            src_ref=slot_block(send_slots, me),
            dst_ref=slot_block(recv_slots, lax.rem(me + n_cols - shift, n_cols)),
            send_sem=slot_send_sem.at[shift],
            recv_sem=slot_recv_sem.at[shift],
            device_id={"cols": left},
        )

    @pl.loop(1, n_cols)
    def _(shift):
        slot_send(shift).start()

    recv_slots[me] = send_slots[me]


    patient = me == 0

    def wait_for_slots():
        @pl.loop(1, n_cols)
        def _(shift):
            slot_receive(shift).wait_recv()

    pl.when(patient)(wait_for_slots)

    @pl.loop(0, fields)
    def _(field):
        row_copy(1, field).start()

    @pl.loop(0, fields)
    def _(field):
        row_copy(2, field).start()

    @pl.loop(0, fields)
    def _(field):
        row_copy(3, field).start()

    def add_panels():
        pl.when(jnp.logical_not(patient))(wait_for_slots)
        rest = recv_slots[:, cap : cap + short, :]
        if fold == 2:
            upper = pltpu.roll(rest.reshape(n_cols * short, 128), 64, 1)
            rest = jnp.concatenate([rest, upper.reshape(n_cols, short, 128)], axis=1)
        received = jnp.concatenate(
            [recv_slots[:, 0:cap, :].reshape(slots, 128), rest.reshape(slots, 128)], axis=1
        )
        target = received[:, field_levels : field_levels + 1].astype(jnp.int32) - 1
        parts = pieces(jnp.transpose(received)[0:field_levels, :])
        for x in range(rows):
            y = lax.broadcasted_iota(jnp.int32, (slots, cells), 1) + x * cells
            hit = (target == y).astype(jnp.float32).astype(jnp.bfloat16)
            increment[x] = sum(
                jnp.dot(part, hit, preferred_element_type=jnp.float32) for part in parts
            )

    def finish(x, field):
        inside = pl.ds(pl.multiple_of(field * levels, SUB), levels)
        total = state[x, field] + increment[x, inside, :]
        mixed = jnp.dot(
            corr[field],
            spread[x] * total,
            precision=lax.Precision.HIGHEST,
            preferred_element_type=jnp.float32,
        )
        result[x, field] = spread[x] * mixed
        out_copy(x, field).start()

    def out_copy(x, field):
        return pltpu.make_async_copy(result.at[x, field], out_hbm.at[x, field], out_sem.at[x, field])

    for time in range(STEPS):
        if time + rows == STEPS:
            add_panels()
        active = [x for x in reversed(range(rows)) if time + rows - x <= STEPS]

        @pl.loop(0, fields)
        def _(field):
            row_copy(time, field).wait_recv()
            for strip in strips:
                ahead = border[time, field, strip]
                for x in active:
                    later = time + rows - x
                    if x == 0:
                        value = history[later - 2, field, strip]
                    else:
                        value = state[x, field, strip]
                    ahead = advance(x, strip, value, ahead)
                    if x == 0 and later < STEPS:
                        history[later - 1, field, strip] = ahead
                    else:
                        state[x, field, strip] = ahead
            if time + rows < STEPS:
                row_copy(time + rows, field).start()
            else:
                finish(time + rows - STEPS, field)

    @pl.loop(1, n_cols)
    def _(shift):
        slot_send(shift).wait_send()

    for time in range(STEPS):

        @pl.loop(0, fields)
        def _(field):
            row_copy(time, field).wait_send()

    for x in range(rows):

        @pl.loop(0, fields)
        def _(field):
            out_copy(x, field).wait()


def per_device(
    adj_in,
    courant_x,
    courant_y,
    spread,
    corr_band,
    jacobian,
    departures,
    obs_owner,
    obs_cell,
    obs_count,
):
    rows, fields, levels, cells = adj_in.shape
    panels, field_levels, channels = jacobian.shape
    n_cols = lax.axis_size("cols")
    cap = -(-(2 * panels // n_cols) // SUB) * SUB
    short = cap // 2 if cap % (2 * SUB) == 0 else cap
    width = -(-(field_levels + 1) // 128) * 128
    anywhere = pl.BlockSpec(memory_space=pl.ANY)
    f32, i32 = jnp.float32, jnp.int32
    return pl.pallas_call(
        functools.partial(window_kernel, n_cols, cap),
        out_shape=jax.ShapeDtypeStruct(adj_in.shape, f32),
        in_specs=[anywhere] * 10,
        out_specs=anywhere,
        scratch_shapes=[
            pltpu.VMEM(adj_in.shape, f32),
            pltpu.VMEM((STEPS - 1, fields, levels, cells), f32),
            pltpu.VMEM((STEPS, fields, levels, cells), f32),
            pltpu.VMEM(courant_x.shape, f32),
            pltpu.VMEM(courant_y.shape, f32),
            pltpu.VMEM(spread.shape, f32),
            pltpu.VMEM(corr_band.shape, f32),
            pltpu.VMEM(jacobian.shape, jacobian.dtype),
            pltpu.VMEM(departures.shape, departures.dtype),
            pltpu.VMEM((1, panels), i32),
            pltpu.VMEM((1, panels), i32),
            pltpu.VMEM((1, panels), i32),
            pltpu.VMEM((panels, channels), f32),
            pltpu.VMEM((panels, width), f32),
            pltpu.VMEM((n_cols, cap + short, 128), f32),
            pltpu.VMEM((n_cols, cap + short, 128), f32),
            pltpu.VMEM((rows, field_levels, cells), f32),
            pltpu.VMEM(adj_in.shape, f32),
            pltpu.SemaphoreType.DMA((rows + 9,)),
            pltpu.SemaphoreType.DMA((STEPS, fields)),
            pltpu.SemaphoreType.DMA((STEPS, fields)),
            pltpu.SemaphoreType.DMA((n_cols,)),
            pltpu.SemaphoreType.DMA((n_cols,)),
            pltpu.SemaphoreType.DMA((rows, fields)),
        ],
        compiler_params=pltpu.CompilerParams(
            collective_id=0, has_side_effects=True, vmem_limit_bytes=48 * 1024 * 1024
        ),
    )(*[pltpu.with_memory_space_constraint(v, pltpu.HBM) for v in (
        adj_in,
        courant_x,
        courant_y,
        spread,
        corr_band,
        jacobian,
        departures,
        obs_owner.reshape(1, panels),
        obs_cell.reshape(1, panels),
        obs_count.reshape(1, panels),
)]
    )


def solution(mesh):
    in_specs = (
        P(("members", "cols"), None, None, None),
        P(("members", "cols"), None, None),
        P(("members", "cols"), None, None),
        P("cols", None, None),
        P(),
        P(("members", "cols"), None, None),
        P(("members", "cols"), None),
        P(("members", "cols")),
        P(("members", "cols")),
        P(("members", "cols")),
    )
    out_specs = P(("members", "cols"), None, None, None)
    return jax.shard_map(
        per_device, mesh=mesh, in_specs=in_specs, out_specs=out_specs, check_vma=False
    )
```
